32 devices in a mesh: groups: 2 (over y), expert: 16 (over z, x, core), sub: 1, pair: 1.
Axes of the slice: x: 2, y: 2, z: 4, core: 2. Of those that a mesh axis runs over, the one named last changes fastest.
Arguments:
- tokens: bfloat16 [128, 3584], P(('groups', 'expert', 'sub', 'pair')), parts along dimension 0, may hold values from -6 to 6
- expert_ids: int32 [128, 8], P(('groups', 'expert', 'sub', 'pair')), parts along dimension 0, may hold values from 0 to 15, all different within a row; in each aligned block of 4 rows (0 to 3, 4 to 7, ...) at most 3 rows name the same one
- scores: float32 [128, 8], P(('groups', 'expert', 'sub', 'pair')), parts along dimension 0, may hold values from 0.05 to 1
- gate_w: bfloat16 [16, 3584, 2048], P('expert', None, 'sub'), may hold values from -0.09375 to 0.09375
- up_w: bfloat16 [16, 3584, 2048], P('expert', None, 'sub'), may hold values from -0.09375 to 0.09375
- down_w: bfloat16 [16, 2048, 3584], P('expert', None, ('sub', 'pair')), may hold values from -0.125 to 0.125
Outputs:
- moe_out: bfloat16 [128, 3584], P(('groups', 'expert', 'sub', 'pair')), parts along dimension 0
The draws below stay inside these ranges and needn't reach their ends.
There are 2 independent parts, one for each index of `groups`. The reference program is written for one: setup_inputs(seed, part) draws one part's arguments, and reference() takes and returns one part's arrays. A program takes and returns all parts, laid end to end along the dimension named above; an argument that names none is the same for every part. Nothing has to cross between parts.
Inputs may be any that keep to these rules, and one draw needn't show every extreme that they name: `expert_ids`: each row names 8 different experts. In each aligned block of 4 rows (the rows of one device) no expert is named by more than 3 rows, a bound that some block reaches.
All inputs are finite; a program needn't handle non-finite values.
Results may differ from the reference program's by a relative error of at most 0.0058.
Values may be sent and summed in bfloat16 or wider, within the bound.
No kernel may reach another device: no remote copies, remote signals or barrier semaphores. Data moves between devices by JAX's collectives and lax.ppermute only.
A program may use at most 128 MiB of HBM per device.

```python
import math
import jax
import jax.numpy as jnp
import numpy as np
from jax import lax

D = 3584
FF = 2048
ROWS_DEV = 4
EXPERTS = 16
TOP = 8
CAP = 3
TOKENS = 64


def block_scale(rng, shape, split, smallest, largest):
    def one(dim, shards_of):
        heights = jax.random.uniform(jax.random.fold_in(jax.random.fold_in(rng, 6), dim), (shards_of,), jnp.float32, smallest / len(split), largest / len(split))
        return jnp.repeat(jnp.exp(heights), shape[dim] // shards_of).reshape((-1,) + (1,) * (len(shape) - dim - 1))

    loudness = one(*split[0])
    for cut in split[1:]:
        loudness = loudness * one(*cut)
    return loudness


def shared_out(stream_key, own, number, rows, amount, top, most, lean):
    ranking = jax.random.permutation(stream_key, amount)
    heavy_load, usual = portions_of(amount, rows * top, most, lean, True), portions_of(amount, rows * top, most, lean, False)
    places = jnp.arange(amount)

    def named(sizes, turn):
        used = int((sizes > 0).sum())
        fixed = max(1, used // 4)
        shifted = fixed + (places - fixed + turn * (used - fixed)) % max(1, amount - fixed)
        return jnp.zeros((amount,), jnp.int32).at[ranking[jnp.where(places < fixed, places, shifted)]].set(jnp.asarray(sizes, jnp.int32))

    sizes = jnp.where(number % 4 == 0, named(heavy_load, number // 4), named(usual, number - number // 4 - 1))
    mixed = jax.random.permutation(jax.random.fold_in(own, 3), amount)
    source_of, receiver = mixed[0:amount // 2 * 2:2], mixed[1:amount // 2 * 2:2]
    margin = jnp.minimum(sizes[source_of] - 1, most - sizes[receiver]) // 2
    margin = jnp.where((source_of == ranking[0]) | (receiver == ranking[0]) | (sizes[receiver] == 0), 0, jnp.maximum(margin, 0))
    shifted = jax.random.randint(jax.random.fold_in(own, 4), (amount // 2,), 0, 1 << 20) % (margin + 1)
    sizes = sizes.at[source_of].add(-shifted).at[receiver].add(shifted)
    labels = jnp.searchsorted(jnp.cumsum(sizes), jnp.arange(rows * top), side="right").astype(jnp.int32)
    table = labels.reshape(top, rows).T
    table = table[jax.random.permutation(jax.random.fold_in(own, 1), rows)]
    turn = jax.random.randint(jax.random.fold_in(own, 2), (rows, 1), 0, top)
    return jnp.take_along_axis(table, (jnp.arange(top)[None, :] + turn) % top, axis=1)


def portions_of(number_of, total, most, skew, full):
    portions = [(1 << 20) // math.isqrt(standing ** skew) + 1 for standing in range(1, number_of + 1)]
    largest = most if full else min(most, max(-(-total // number_of), total * portions[0] // sum(portions)))
    least = 1 if total - largest >= number_of - 1 else 0
    given, spare = [largest] + [least] * (number_of - 1), total - largest - least * (number_of - 1)
    while spare > 0:
        movable = [i for i in range(1, number_of) if given[i] < largest] or [i for i in range(1, number_of) if given[i] < most]
        pool, left = sum([portions[i] for i in movable]), spare
        for i in movable:
            addition = min(most - given[i], max(1, left * portions[i] // pool), spare)
            given[i] = given[i] + addition
            spare = spare - addition
    return np.array(given)


def normal_values(stream_key, shape, width, bound, shards=(), held_as=jnp.bfloat16):
    entries = width * jax.random.normal(stream_key, shape, jnp.float32)
    if shards:
        entries = entries * block_scale(stream_key, shape, shards, -0.22, 0.18)
    return jnp.clip(entries, -bound, bound).astype(held_as)


def setup_inputs(seed: int = 0, part: int = 0) -> dict:
    seeds = jax.random.split(jax.random.key(seed), 7)
    own_keys = jax.random.split(jax.random.fold_in(seeds[6], part), 7)
    tokens = normal_values(own_keys[0], (TOKENS, D), 1.0, 6.0, ((0, 16),))
    expert_ids_keys = jax.random.split(jax.random.fold_in(own_keys[1], 1), TOKENS // ROWS_DEV)
    expert_ids_turns = jax.random.permutation(jax.random.fold_in(own_keys[1], 3), TOKENS // ROWS_DEV)
    expert_ids = jax.vmap(lambda own, number: shared_out(jax.random.fold_in(own_keys[1], 2), own, number, ROWS_DEV, EXPERTS, TOP, CAP, 2))(expert_ids_keys, expert_ids_turns).reshape((TOKENS, TOP))
    scores = jnp.clip(jnp.exp(math.log(1.0) - 2.9957323 * jax.random.uniform(own_keys[2], (TOKENS, TOP), jnp.float32) ** block_scale(own_keys[2], (TOKENS, TOP), ((0, 16),), -0.2, 0.2)), 0.05, 1.0)
    gate_w = normal_values(seeds[3], (EXPERTS, D, FF), D ** -0.5, 0.09375, ((0, 16),))
    up_w = normal_values(seeds[4], (EXPERTS, D, FF), D ** -0.5, 0.09375, ((0, 16),))
    down_w = normal_values(seeds[5], (EXPERTS, FF, D), FF ** -0.5, 0.125, ((0, 16),))
    return {"tokens": tokens, "expert_ids": expert_ids, "scores": scores, "gate_w": gate_w, "up_w": up_w, "down_w": down_w}


def slot_table(ids, count):
    hit = (ids[:, :, None] == jnp.arange(count, dtype=jnp.int32)[None, None, :]).astype(jnp.int32)
    per_row = jnp.sum(hit, axis=1)
    before = jnp.cumsum(per_row, axis=0) - per_row
    slot = jnp.sum(hit * before[:, None, :], axis=2)
    return slot


def reference(tokens, expert_ids, scores, gate_w, up_w, down_w):
    sources = TOKENS // ROWS_DEV
    blocks = expert_ids.reshape(sources, ROWS_DEV, TOP)
    slot = jax.vmap(lambda block_ids: slot_table(block_ids, EXPERTS))(blocks)
    base = (jnp.arange(sources, dtype=jnp.int32) * CAP)[:, None, None]
    position = (base + slot).reshape(TOKENS, TOP).astype(jnp.int32)
    weight = 2.5 * scores / jnp.sum(scores, axis=1, keepdims=True)
    padded = jnp.concatenate([tokens, jnp.zeros((1, D), jnp.bfloat16)], axis=0)
    row_index = jnp.broadcast_to(jnp.arange(TOKENS, dtype=jnp.int32)[:, None], (TOKENS, TOP))

    def one_expert(total, packed):
        index, wg, wu, wd = packed
        mine = expert_ids == index
        target = jnp.where(mine, position, sources * CAP).astype(jnp.int32)
        source_row = jnp.full((sources * CAP,), TOKENS, jnp.int32)
        source_row = source_row.at[target.reshape(-1)].set(row_index.reshape(-1), mode="drop")
        bucket = padded[source_row]
        gate_part = jnp.dot(bucket, wg, preferred_element_type=jnp.float32)
        up_part = jnp.dot(bucket, wu, preferred_element_type=jnp.float32)
        hidden = (jax.nn.silu(gate_part) * up_part).astype(jnp.bfloat16)
        result = jnp.dot(hidden, wd, preferred_element_type=jnp.float32).astype(jnp.bfloat16)
        picked = result[jnp.where(mine, position, 0).astype(jnp.int32)].astype(jnp.float32)
        scale = jnp.where(mine, weight, jnp.float32(0.0))
        return total + jnp.sum(scale[:, :, None] * picked, axis=1), None

    start = jnp.zeros((TOKENS, D), jnp.float32)
    total, _ = lax.scan(one_expert, start, (jnp.arange(EXPERTS, dtype=jnp.int32), gate_w, up_w, down_w))
    return total.astype(jnp.bfloat16)
```

```python
import jax
import jax.numpy as jnp
from jax import lax
from jax.experimental import pallas as pl
from jax.experimental.pallas import tpu as pltpu
from jax.sharding import PartitionSpec as P

LANES = 128


def slot_table(ids, count):
    hit = (ids[:, :, None] == jnp.arange(count, dtype=jnp.int32)[None, None, :]).astype(jnp.int32)
    per_row = jnp.sum(hit, axis=1)
    before = jnp.cumsum(per_row, axis=0) - per_row
    slot = jnp.sum(hit * before[:, None, :], axis=2)
    return (hit, slot)


def general_shards(tokens, expert_ids, scores, gate_w, up_w, down_w):
    experts = lax.axis_size("expert")
    sub_count = lax.axis_size("sub")
    pair_count = lax.axis_size("pair")
    sharers = sub_count * pair_count
    row_count = tokens.shape[0]
    top_k = expert_ids.shape[1]
    model_width = tokens.shape[1]
    capacity = min(row_count, row_count * top_k // experts + 1)
    weight_gate = gate_w[0]
    weight_up = up_w[0]
    weight_down = down_w[0]
    unit_count = weight_gate.shape[1]
    slot_range = jnp.arange(capacity, dtype=jnp.int32)
    hit, slot = slot_table(expert_ids, experts)
    in_slot = (slot[:, :, None] == slot_range[None, None, :]).astype(jnp.int32)
    place = jnp.sum(hit[:, :, :, None] * in_slot[:, :, None, :], axis=1).astype(jnp.bfloat16)
    buckets = jnp.einsum("rec,rd->ecd", place, tokens, preferred_element_type=jnp.float32).astype(
        jnp.bfloat16
    )
    received = lax.all_to_all(buckets, "expert", split_axis=0, concat_axis=0, tiled=True)
    flat = received.reshape(experts * capacity, model_width)
    piece = lax.all_gather(flat, "sub", axis=0, tiled=True)
    gate_part = jnp.dot(piece, weight_gate, preferred_element_type=jnp.float32)
    up_part = jnp.dot(piece, weight_up, preferred_element_type=jnp.float32)
    hidden = (jax.nn.silu(gate_part) * up_part).astype(jnp.bfloat16)
    stacked = hidden.reshape(sub_count, 1, experts * capacity, unit_count)
    joined = lax.all_gather(stacked, "pair", axis=1, tiled=True)
    joined = joined.reshape(sharers * experts * capacity, unit_count)
    outputs = jnp.dot(
        lax.all_gather(joined, "sub", axis=1, tiled=True),
        weight_down,
        preferred_element_type=jnp.float32,
    ).astype(jnp.bfloat16)
    outputs = outputs.reshape(sharers, experts, capacity, weight_down.shape[1])
    back = lax.all_to_all(
        lax.all_to_all(outputs, ("sub", "pair"), split_axis=0, concat_axis=3, tiled=True),
        "expert",
        split_axis=1,
        concat_axis=0,
        tiled=True,
    )
    back = back.reshape(experts, capacity, model_width).astype(jnp.float32)
    weight = 2.5 * scores / jnp.sum(scores, axis=1, keepdims=True)
    spread = weight[:, :, None, None] * (hit[:, :, :, None] * in_slot[:, :, None, :]).astype(
        jnp.float32
    )
    mixing = jnp.sum(spread, axis=1)
    total = jnp.einsum(
        "rec,ecd->rd",
        mixing,
        back,
        precision=lax.Precision.HIGHEST,
        preferred_element_type=jnp.float32,
    )
    return total.astype(jnp.bfloat16)


def swap(x, distance):
    count = lax.axis_size("expert")
    return lax.ppermute(x, "expert", [(i, i ^ distance) for i in range(count)])


def vmem(count):
    return [pl.BlockSpec(memory_space=pltpu.VMEM)] * count


def pack_kernel(experts, tokens_ref, ids_ref, scores_ref, out_ref):
    width = tokens_ref.shape[1]
    scores = scores_ref[...]
    ids = ids_ref[...]
    weight = 2.5 * scores / jnp.sum(scores, axis=1, keepdims=True)
    lane = lax.broadcasted_iota(jnp.int32, (scores.shape[0], LANES), 1)
    target = lax.rem(lane, experts)
    dense = jnp.zeros((scores.shape[0], LANES), jnp.float32)
    for k in range(scores.shape[1]):
        dense = dense + jnp.where(ids[:, k : k + 1] == target, weight[:, k : k + 1], 0.0)
    high = dense.astype(jnp.bfloat16).astype(jnp.float32)
    both = jnp.where(lane < experts, high, jnp.where(lane < 2 * experts, dense - high, 0.0))
    out_ref[:, :width] = tokens_ref[...]
    out_ref[:, width:] = both.astype(jnp.bfloat16)


def hidden_kernel(step, xa_ref, xb_ref, gate_ref, up_ref, out_ref):
    width = gate_ref.shape[1]
    x = jnp.concatenate([xa_ref[:, :width], xb_ref[:, :width]], axis=0)
    for start in range(0, gate_ref.shape[2], step):
        cut = slice(start, start + step)
        gate = jnp.dot(x, gate_ref[0, :, cut], preferred_element_type=jnp.float32)
        up = jnp.dot(x, up_ref[0, :, cut], preferred_element_type=jnp.float32)
        out_ref[:, cut] = (gate / (1.0 + jnp.exp(-gate)) * up).astype(jnp.bfloat16)


def down_kernel(step, experts, hidden_ref, xa_ref, xb_ref, down_ref, keep_ref, send_ref):
    width = down_ref.shape[2]
    half = keep_ref.shape[0]
    me = lax.axis_index("expert")
    hidden = hidden_ref[...]
    spread = jnp.concatenate([xa_ref[:, width:], xb_ref[:, width:]], axis=0).astype(jnp.float32)
    lane = lax.broadcasted_iota(jnp.int32, spread.shape, 1)
    mine = (lane == me) | (lane == me + experts)
    weight = jnp.sum(jnp.where(mine, spread, 0.0), axis=1, keepdims=True)
    for start in range(0, width, step):
        cut = slice(start, start + step)
        out = jnp.dot(hidden, down_ref[0, :, cut], preferred_element_type=jnp.float32)
        part = out.astype(jnp.bfloat16).astype(jnp.float32) * weight
        keep_ref[:, cut] = part[:half].astype(keep_ref.dtype)
        send_ref[:, cut] = part[half:].astype(send_ref.dtype)


def add_kernel(kept_ref, got_ref, keep_ref, send_ref):
    half = keep_ref.shape[0]
    total = kept_ref[...] + got_ref[...].astype(jnp.float32)
    keep_ref[...] = total[:half]
    send_ref[...] = total[half:].astype(send_ref.dtype)


def last_kernel(kept_ref, got_ref, out_ref):
    out_ref[...] = (kept_ref[...] + got_ref[...].astype(jnp.float32)).astype(out_ref.dtype)


def shards(tokens, expert_ids, scores, gate_w, up_w, down_w):
    experts = lax.axis_size("expert")
    rows, width = tokens.shape
    units = gate_w.shape[2]
    params = pltpu.CompilerParams(vmem_limit_bytes=6 * 2**20)
    gate_w = pltpu.with_memory_space_constraint(gate_w, pltpu.VMEM)
    up_w = pltpu.with_memory_space_constraint(up_w, pltpu.VMEM)
    down_w = pltpu.with_memory_space_constraint(down_w, pltpu.VMEM)
    held = pl.pallas_call(
        lambda *refs: pack_kernel(experts, *refs),
        out_shape=jax.ShapeDtypeStruct((rows, width + LANES), jnp.bfloat16),
        in_specs=vmem(3),
        out_specs=vmem(1)[0],
        compiler_params=params,
        cost_estimate=pl.CostEstimate(flops=40_000_000_000, bytes_accessed=100_000_000, transcendentals=0),
        name="pack",
    )(tokens, expert_ids, scores)
    distance = experts // 2
    while distance > 1:
        held = jnp.concatenate([held, swap(held, distance)], axis=0)
        distance //= 2
    other = swap(held, 1)
    half = held.shape[0]
    hidden = pl.pallas_call(
        lambda *refs: hidden_kernel(256, *refs),
        out_shape=jax.ShapeDtypeStruct((2 * half, units), jnp.bfloat16),
        in_specs=vmem(4),
        out_specs=vmem(1)[0],
        compiler_params=params,
        name="hidden",
    )(held, other, gate_w, up_w)
    keep, send = pl.pallas_call(
        lambda *refs: down_kernel(256, experts, *refs),
        out_shape=[
            jax.ShapeDtypeStruct((half, width), jnp.float32),
            jax.ShapeDtypeStruct((half, width), jnp.bfloat16),
        ],
        in_specs=vmem(4),
        out_specs=vmem(2),
        compiler_params=params,
        name="down",
    )(hidden, held, other, down_w)
    distance = 1
    while distance < experts // 2:
        got = swap(send, distance)
        half //= 2
        keep, send = pl.pallas_call(
            add_kernel,
            out_shape=[
                jax.ShapeDtypeStruct((half, width), jnp.float32),
                jax.ShapeDtypeStruct((half, width), jnp.bfloat16),
            ],
            in_specs=vmem(2),
            out_specs=vmem(2),
            compiler_params=params,
            name="add",
        )(keep, got)
        distance *= 2
    got = swap(send, distance)
    return pl.pallas_call(
        last_kernel,
        out_shape=jax.ShapeDtypeStruct((rows, width), jnp.bfloat16),
        in_specs=vmem(2),
        out_specs=vmem(1)[0],
        compiler_params=params,
        name="last",
    )(keep, got)


def solution(mesh):
    in_specs = (
        P(("groups", "expert", "sub", "pair"), None),
        P(("groups", "expert", "sub", "pair"), None),
        P(("groups", "expert", "sub", "pair"), None),
        P("expert", None, "sub"),
        P("expert", None, "sub"),
        P("expert", None, ("sub", "pair")),
    )
    out_specs = P(("groups", "expert", "sub", "pair"), None)
    whole = mesh.shape["sub"] == 1 and mesh.shape["pair"] == 1
    body = shards if whole else general_shards
    return jax.shard_map(body, mesh=mesh, in_specs=in_specs, out_specs=out_specs, check_vma=False)
```

```python
import jax
import jax.numpy as jnp
from jax import lax
from jax.experimental import pallas as pl
from jax.experimental.pallas import tpu as pltpu
from jax.sharding import PartitionSpec as P

LANES = 128


def slot_table(ids, count):
    hit = (ids[:, :, None] == jnp.arange(count, dtype=jnp.int32)[None, None, :]).astype(jnp.int32)
    per_row = jnp.sum(hit, axis=1)
    before = jnp.cumsum(per_row, axis=0) - per_row
    slot = jnp.sum(hit * before[:, None, :], axis=2)
    return (hit, slot)


def general_shards(tokens, expert_ids, scores, gate_w, up_w, down_w):
    experts = lax.axis_size("expert")
    sub_count = lax.axis_size("sub")
    pair_count = lax.axis_size("pair")
    sharers = sub_count * pair_count
    row_count = tokens.shape[0]
    top_k = expert_ids.shape[1]
    model_width = tokens.shape[1]
    capacity = min(row_count, row_count * top_k // experts + 1)
    weight_gate = gate_w[0]
    weight_up = up_w[0]
    weight_down = down_w[0]
    unit_count = weight_gate.shape[1]
    slot_range = jnp.arange(capacity, dtype=jnp.int32)
    hit, slot = slot_table(expert_ids, experts)
    in_slot = (slot[:, :, None] == slot_range[None, None, :]).astype(jnp.int32)
    place = jnp.sum(hit[:, :, :, None] * in_slot[:, :, None, :], axis=1).astype(jnp.bfloat16)
    buckets = jnp.einsum("rec,rd->ecd", place, tokens, preferred_element_type=jnp.float32).astype(
        jnp.bfloat16
    )
    received = lax.all_to_all(buckets, "expert", split_axis=0, concat_axis=0, tiled=True)
    flat = received.reshape(experts * capacity, model_width)
    piece = lax.all_gather(flat, "sub", axis=0, tiled=True)
    gate_part = jnp.dot(piece, weight_gate, preferred_element_type=jnp.float32)
    up_part = jnp.dot(piece, weight_up, preferred_element_type=jnp.float32)
    hidden = (jax.nn.silu(gate_part) * up_part).astype(jnp.bfloat16)
    stacked = hidden.reshape(sub_count, 1, experts * capacity, unit_count)
    joined = lax.all_gather(stacked, "pair", axis=1, tiled=True)
    joined = joined.reshape(sharers * experts * capacity, unit_count)
    outputs = jnp.dot(
        lax.all_gather(joined, "sub", axis=1, tiled=True),
        weight_down,
        preferred_element_type=jnp.float32,
    ).astype(jnp.bfloat16)
    outputs = outputs.reshape(sharers, experts, capacity, weight_down.shape[1])
    back = lax.all_to_all(
        lax.all_to_all(outputs, ("sub", "pair"), split_axis=0, concat_axis=3, tiled=True),
        "expert",
        split_axis=1,
        concat_axis=0,
        tiled=True,
    )
    back = back.reshape(experts, capacity, model_width).astype(jnp.float32)
    weight = 2.5 * scores / jnp.sum(scores, axis=1, keepdims=True)
    spread = weight[:, :, None, None] * (hit[:, :, :, None] * in_slot[:, :, None, :]).astype(
        jnp.float32
    )
    mixing = jnp.sum(spread, axis=1)
    total = jnp.einsum(
        "rec,ecd->rd",
        mixing,
        back,
        precision=lax.Precision.HIGHEST,
        preferred_element_type=jnp.float32,
    )
    return total.astype(jnp.bfloat16)


def swap(x, distance):
    count = lax.axis_size("expert")
    return lax.ppermute(x, "expert", [(i, i ^ distance) for i in range(count)])


def vmem(count):
    return [pl.BlockSpec(memory_space=pltpu.VMEM)] * count


def hbm(count):
    return [pl.BlockSpec(memory_space=pltpu.HBM)] * count


def filled(x, rows):
    return jnp.concatenate([x, jnp.zeros((rows - x.shape[0], x.shape[1]), x.dtype)], axis=0)


def pack_kernel(experts, tokens_ref, ids_ref, scores_ref, out_ref, ids_vmem, scores_vmem, sems):
    width = tokens_ref.shape[1]
    ids_copy = pltpu.make_async_copy(ids_ref, ids_vmem, sems.at[0])
    scores_copy = pltpu.make_async_copy(scores_ref, scores_vmem, sems.at[1])
    tokens_copy = pltpu.make_async_copy(tokens_ref, out_ref.at[:, pl.ds(0, width)], sems.at[2])
    ids_copy.start()
    scores_copy.start()
    tokens_copy.start()
    ids_copy.wait()
    scores_copy.wait()
    scores = scores_vmem[...]
    ids = ids_vmem[...]
    weight = 2.5 * scores / jnp.sum(scores, axis=1, keepdims=True)
    lane = lax.broadcasted_iota(jnp.int32, (scores.shape[0], LANES), 1)
    target = lax.rem(lane, experts)
    dense = jnp.zeros((scores.shape[0], LANES), jnp.float32)
    for k in range(scores.shape[1]):
        dense = dense + jnp.where(ids[:, k : k + 1] == target, weight[:, k : k + 1], 0.0)
    high = dense.astype(jnp.bfloat16).astype(jnp.float32)
    both = jnp.where(lane < experts, high, jnp.where(lane < 2 * experts, dense - high, 0.0))
    out_ref[:, width:] = both.astype(jnp.bfloat16)
    tokens_copy.wait()


def join_kernel(*refs):
    out_ref = refs[-1]
    pieces = [ref[...].astype(jnp.float32) for ref in refs[:-1]]
    out_ref[...] = jnp.concatenate(pieces, axis=0).astype(out_ref.dtype)


def join(pieces, params):
    rows = sum(piece.shape[0] for piece in pieces)
    return pl.pallas_call(
        join_kernel,
        out_shape=jax.ShapeDtypeStruct((rows, pieces[0].shape[1]), pieces[0].dtype),
        in_specs=vmem(len(pieces)),
        out_specs=vmem(1)[0],
        compiler_params=params,
        name="join",
    )(*pieces)


def hidden_kernel(step, fill, xa_ref, xb_ref, gate_ref, up_ref, out_ref):
    width = gate_ref.shape[1]
    rows = out_ref.shape[0]
    x = filled(jnp.concatenate([xa_ref[:, :width], xb_ref[:, :width]], axis=0), fill)
    for start in range(0, gate_ref.shape[2], step):
        cut = slice(start, start + step)
        gate = jnp.dot(x, gate_ref[0, :, cut], preferred_element_type=jnp.float32)[:rows]
        up = jnp.dot(x, up_ref[0, :, cut], preferred_element_type=jnp.float32)[:rows]
        out_ref[:, cut] = (gate / (1.0 + jnp.exp(-gate)) * up).astype(jnp.bfloat16)


def down_kernel(step, fill, experts, hidden_ref, xa_ref, xb_ref, down_ref, keep_ref, send_ref):
    width = down_ref.shape[2]
    half = keep_ref.shape[0]
    me = lax.axis_index("expert")
    hidden = filled(hidden_ref[...], fill)
    spread = jnp.concatenate([xa_ref[:, width:], xb_ref[:, width:]], axis=0).astype(jnp.float32)
    lane = lax.broadcasted_iota(jnp.int32, spread.shape, 1)
    mine = (lane == me) | (lane == me + experts)
    weight = jnp.sum(jnp.where(mine, spread, 0.0), axis=1, keepdims=True)
    for start in range(0, width, step):
        cut = slice(start, start + step)
        out = jnp.dot(hidden, down_ref[0, :, cut], preferred_element_type=jnp.float32)[: 2 * half]
        part = out.astype(jnp.bfloat16).astype(jnp.float32) * weight
        keep_ref[:, cut] = part[:half]
        send_ref[:, cut] = part[half:].astype(send_ref.dtype)


def first_add_kernel(kept_ref, got_ref, keep_ref, *send_refs):
    total = kept_ref[...] + got_ref[...].astype(jnp.float32)
    rows = keep_ref.shape[0]
    keep_ref[...] = total[:rows]
    for i, send_ref in enumerate(send_refs):
        send_ref[...] = total[(i + 1) * rows : (i + 2) * rows].astype(send_ref.dtype)


def second_add_kernel(kept_ref, *refs):
    got_refs, (keep_ref, send_ref) = refs[:-2], refs[-2:]
    total = kept_ref[...]
    for got_ref in got_refs:
        total = total + got_ref[...].astype(jnp.float32)
    half = keep_ref.shape[0]
    keep_ref[...] = total[:half]
    send_ref[...] = total[half:].astype(send_ref.dtype)


def last_kernel(kept_ref, got_ref, out_ref):
    out_ref[...] = (kept_ref[...] + got_ref[...].astype(jnp.float32)).astype(out_ref.dtype)


def shards(tokens, expert_ids, scores, gate_w, up_w, down_w):
    experts = lax.axis_size("expert")
    rows, width = tokens.shape
    units = gate_w.shape[2]
    far = experts // 2
    middle = [d for d in range(far - 2, 0, -2)]
    half = rows * far
    fill = max(2 * half, 128)
    params = pltpu.CompilerParams(vmem_limit_bytes=6 * 2**20)
    gate_w = pltpu.with_memory_space_constraint(gate_w, pltpu.VMEM)
    up_w = pltpu.with_memory_space_constraint(up_w, pltpu.VMEM)
    down_w = pltpu.with_memory_space_constraint(down_w, pltpu.VMEM)
    tokens, expert_ids, scores = [
        pltpu.with_memory_space_constraint(x, pltpu.HBM) for x in (tokens, expert_ids, scores)
    ]
    packed = pl.pallas_call(
        lambda *refs: pack_kernel(experts, *refs),
        out_shape=jax.ShapeDtypeStruct((rows, width + LANES), jnp.bfloat16),
        in_specs=hbm(3),
        out_specs=vmem(1)[0],
        scratch_shapes=[
            pltpu.VMEM(expert_ids.shape, expert_ids.dtype),
            pltpu.VMEM(scores.shape, scores.dtype),
            pltpu.SemaphoreType.DMA((3,)),
        ],
        compiler_params=params,
        cost_estimate=pl.CostEstimate(
            flops=40_000_000_000, bytes_accessed=100_000_000, transcendentals=0
        ),
        name="pack",
    )(tokens, expert_ids, scores)
    near = join([packed, swap(packed, far)], params)
    held = join([near] + [swap(near, d) for d in middle], params)
    other = swap(held, 1)
    hidden = pl.pallas_call(
        lambda *refs: hidden_kernel(256, fill, *refs),
        out_shape=jax.ShapeDtypeStruct((2 * half, units), jnp.bfloat16),
        in_specs=vmem(4),
        out_specs=vmem(1)[0],
        compiler_params=params,
        name="hidden",
    )(held, other, gate_w, up_w)
    keep, send = pl.pallas_call(
        lambda *refs: down_kernel(256, fill, experts, *refs),
        out_shape=[
            jax.ShapeDtypeStruct((half, width), jnp.float32),
            jax.ShapeDtypeStruct((half, width), jnp.bfloat16),
        ],
        in_specs=vmem(4),
        out_specs=vmem(2),
        compiler_params=params,
        name="down",
    )(hidden, held, other, down_w)
    got = swap(send, 1)
    keep, *sends = pl.pallas_call(
        first_add_kernel,
        out_shape=[jax.ShapeDtypeStruct((2 * rows, width), jnp.float32)]
        + [jax.ShapeDtypeStruct((2 * rows, width), jnp.bfloat16)] * len(middle),
        in_specs=vmem(2),
        out_specs=vmem(1 + len(middle)),
        compiler_params=params,
        name="first_add",
    )(keep, got)
    gots = [swap(send, d) for send, d in zip(sends, middle)]
    keep, send = pl.pallas_call(
        second_add_kernel,
        out_shape=[
            jax.ShapeDtypeStruct((rows, width), jnp.float32),
            jax.ShapeDtypeStruct((rows, width), jnp.bfloat16),
        ],
        in_specs=vmem(1 + len(middle)),
        out_specs=vmem(2),
        compiler_params=params,
        name="second_add",
    )(keep, *gots)
    got = swap(send, far)
    return pl.pallas_call(
        last_kernel,
        out_shape=jax.ShapeDtypeStruct((rows, width), jnp.bfloat16),
        in_specs=vmem(2),
        out_specs=vmem(1)[0],
        compiler_params=params,
        name="last",
    )(keep, got)


def solution(mesh):
    in_specs = (
        P(("groups", "expert", "sub", "pair"), None),
        P(("groups", "expert", "sub", "pair"), None),
        P(("groups", "expert", "sub", "pair"), None),
        P("expert", None, "sub"),
        P("expert", None, "sub"),
        P("expert", None, ("sub", "pair")),
    )
    out_specs = P(("groups", "expert", "sub", "pair"), None)
    whole = mesh.shape["sub"] == 1 and mesh.shape["pair"] == 1 and mesh.shape["expert"] == 16
    body = shards if whole else general_shards
    return jax.shard_map(body, mesh=mesh, in_specs=in_specs, out_specs=out_specs, check_vma=False)
```

```python
import jax
import jax.numpy as jnp
from jax import lax
from jax.experimental import pallas as pl
from jax.experimental.pallas import tpu as pltpu
from jax.sharding import PartitionSpec as P

LANES = 128
PARTS = 1


def slot_table(ids, count):
    hit = (ids[:, :, None] == jnp.arange(count, dtype=jnp.int32)[None, None, :]).astype(jnp.int32)
    per_row = jnp.sum(hit, axis=1)
    before = jnp.cumsum(per_row, axis=0) - per_row
    slot = jnp.sum(hit * before[:, None, :], axis=2)
    return (hit, slot)


def general_shards(tokens, expert_ids, scores, gate_w, up_w, down_w):
    experts = lax.axis_size("expert")
    sub_count = lax.axis_size("sub")
    pair_count = lax.axis_size("pair")
    sharers = sub_count * pair_count
    row_count = tokens.shape[0]
    top_k = expert_ids.shape[1]
    model_width = tokens.shape[1]
    capacity = min(row_count, row_count * top_k // experts + 1)
    weight_gate = gate_w[0]
    weight_up = up_w[0]
    weight_down = down_w[0]
    unit_count = weight_gate.shape[1]
    slot_range = jnp.arange(capacity, dtype=jnp.int32)
    hit, slot = slot_table(expert_ids, experts)
    in_slot = (slot[:, :, None] == slot_range[None, None, :]).astype(jnp.int32)
    place = jnp.sum(hit[:, :, :, None] * in_slot[:, :, None, :], axis=1).astype(jnp.bfloat16)
    buckets = jnp.einsum("rec,rd->ecd", place, tokens, preferred_element_type=jnp.float32).astype(
        jnp.bfloat16
    )
    received = lax.all_to_all(buckets, "expert", split_axis=0, concat_axis=0, tiled=True)
    flat = received.reshape(experts * capacity, model_width)
    piece = lax.all_gather(flat, "sub", axis=0, tiled=True)
    gate_part = jnp.dot(piece, weight_gate, preferred_element_type=jnp.float32)
    up_part = jnp.dot(piece, weight_up, preferred_element_type=jnp.float32)
    hidden = (jax.nn.silu(gate_part) * up_part).astype(jnp.bfloat16)
    stacked = hidden.reshape(sub_count, 1, experts * capacity, unit_count)
    joined = lax.all_gather(stacked, "pair", axis=1, tiled=True)
    joined = joined.reshape(sharers * experts * capacity, unit_count)
    outputs = jnp.dot(
        lax.all_gather(joined, "sub", axis=1, tiled=True),
        weight_down,
        preferred_element_type=jnp.float32,
    ).astype(jnp.bfloat16)
    outputs = outputs.reshape(sharers, experts, capacity, weight_down.shape[1])
    back = lax.all_to_all(
        lax.all_to_all(outputs, ("sub", "pair"), split_axis=0, concat_axis=3, tiled=True),
        "expert",
        split_axis=1,
        concat_axis=0,
        tiled=True,
    )
    back = back.reshape(experts, capacity, model_width).astype(jnp.float32)
    weight = 2.5 * scores / jnp.sum(scores, axis=1, keepdims=True)
    spread = weight[:, :, None, None] * (hit[:, :, :, None] * in_slot[:, :, None, :]).astype(
        jnp.float32
    )
    mixing = jnp.sum(spread, axis=1)
    total = jnp.einsum(
        "rec,ecd->rd",
        mixing,
        back,
        precision=lax.Precision.HIGHEST,
        preferred_element_type=jnp.float32,
    )
    return total.astype(jnp.bfloat16)


def swap(x, distance):
    count = lax.axis_size("expert")
    return lax.ppermute(x, "expert", [(i, i ^ distance) for i in range(count)])


def vmem(count):
    return [pl.BlockSpec(memory_space=pltpu.VMEM)] * count


def hbm(count):
    return [pl.BlockSpec(memory_space=pltpu.HBM)] * count


def filled(x, rows):
    return jnp.concatenate([x, jnp.zeros((rows - x.shape[0], x.shape[1]), x.dtype)], axis=0)


def pack_kernel(experts, tokens_ref, ids_ref, scores_ref, out_ref, ids_vmem, scores_vmem, sems):
    width = tokens_ref.shape[1]
    ids_copy = pltpu.make_async_copy(ids_ref, ids_vmem, sems.at[0])
    scores_copy = pltpu.make_async_copy(scores_ref, scores_vmem, sems.at[1])
    tokens_copy = pltpu.make_async_copy(tokens_ref, out_ref.at[:, pl.ds(0, width)], sems.at[2])
    ids_copy.start()
    scores_copy.start()
    tokens_copy.start()
    ids_copy.wait()
    scores_copy.wait()
    scores = scores_vmem[...]
    ids = ids_vmem[...]
    weight = 2.5 * scores / jnp.sum(scores, axis=1, keepdims=True)
    lane = lax.broadcasted_iota(jnp.int32, (scores.shape[0], LANES), 1)
    target = lax.rem(lane, experts)
    dense = jnp.zeros((scores.shape[0], LANES), jnp.float32)
    for k in range(scores.shape[1]):
        dense = dense + jnp.where(ids[:, k : k + 1] == target, weight[:, k : k + 1], 0.0)
    high = dense.astype(jnp.bfloat16).astype(jnp.float32)
    both = jnp.where(lane < experts, high, jnp.where(lane < 2 * experts, dense - high, 0.0))
    out_ref[:, width:] = both.astype(jnp.bfloat16)
    tokens_copy.wait()


def join_kernel(*refs):
    out_ref = refs[-1]
    pieces = [ref[...].astype(jnp.float32) for ref in refs[:-1]]
    out_ref[...] = jnp.concatenate(pieces, axis=0).astype(out_ref.dtype)


def join(pieces, params):
    rows = sum(piece.shape[0] for piece in pieces)
    return pl.pallas_call(
        join_kernel,
        out_shape=jax.ShapeDtypeStruct((rows, pieces[0].shape[1]), pieces[0].dtype),
        in_specs=vmem(len(pieces)),
        out_specs=vmem(1)[0],
        compiler_params=params,
        name="join",
    )(*pieces)


def hidden_kernel(step, fill, experts, *refs):
    *x_refs, gate_ref, up_ref, out_ref, weight_ref = refs
    width = gate_ref.shape[1]
    rows = out_ref.shape[0]
    me = lax.axis_index("expert")
    spread = jnp.concatenate([ref[:, width:].astype(jnp.float32) for ref in x_refs], axis=0)
    lane = lax.broadcasted_iota(jnp.int32, spread.shape, 1)
    mine = (lane == me) | (lane == me + experts)
    weight = jnp.sum(jnp.where(mine, spread, 0.0), axis=1, keepdims=True)
    weight_ref[...] = jnp.broadcast_to(weight, weight_ref.shape)
    x = jnp.concatenate([ref[:, :width].astype(jnp.float32) for ref in x_refs], axis=0)
    x = filled(x.astype(jnp.bfloat16), fill)
    for start in range(0, gate_ref.shape[2], step):
        cut = slice(start, start + step)
        gate = jnp.dot(x, gate_ref[0, :, cut], preferred_element_type=jnp.float32)[:rows]
        up = jnp.dot(x, up_ref[0, :, cut], preferred_element_type=jnp.float32)[:rows]
        out_ref[:, cut] = (gate / (1.0 + jnp.exp(-gate)) * up).astype(jnp.bfloat16)


def down_kernel(step, fill, base, hidden_ref, weight_ref, down_ref, keep_ref, send_ref):
    half, width = keep_ref.shape
    hidden = filled(hidden_ref[...], fill)
    weight = weight_ref[:, :1]
    for start in range(0, width, step):
        cut = slice(start, start + step)
        columns = slice(base + start, base + start + step)
        out = jnp.dot(hidden, down_ref[0, :, columns], preferred_element_type=jnp.float32)
        part = out[: 2 * half].astype(jnp.bfloat16).astype(jnp.float32) * weight
        keep_ref[:, cut] = part[:half]
        send_ref[:, cut] = part[half:].astype(send_ref.dtype)


def first_add_kernel(parts, *refs):
    kept_refs, got_refs = refs[:parts], refs[parts : 2 * parts]
    keep_ref, *send_refs = refs[2 * parts :]
    rows = keep_ref.shape[0]
    base = 0
    for kept_ref, got_ref in zip(kept_refs, got_refs):
        cut = slice(base, base + kept_ref.shape[1])
        base += kept_ref.shape[1]
        total = kept_ref[...] + got_ref[...].astype(jnp.float32)
        keep_ref[:, cut] = total[:rows]
        for i, send_ref in enumerate(send_refs):
            send_ref[:, cut] = total[(i + 1) * rows : (i + 2) * rows].astype(send_ref.dtype)


def second_add_kernel(kept_ref, *refs):
    got_refs, (keep_ref, send_ref) = refs[:-2], refs[-2:]
    total = kept_ref[...]
    for got_ref in got_refs:
        total = total + got_ref[...].astype(jnp.float32)
    half = keep_ref.shape[0]
    keep_ref[...] = total[:half]
    send_ref[...] = total[half:].astype(send_ref.dtype)


def last_kernel(kept_ref, got_ref, out_ref):
    out_ref[...] = (kept_ref[...] + got_ref[...].astype(jnp.float32)).astype(out_ref.dtype)


def shards(tokens, expert_ids, scores, gate_w, up_w, down_w):
    experts = lax.axis_size("expert")
    rows, width = tokens.shape
    units = gate_w.shape[2]
    far = experts // 2
    middle = [d for d in range(2, far, 2)]
    half = rows * far
    fill = max(2 * half, 128)
    params = pltpu.CompilerParams(vmem_limit_bytes=6 * 2**20)
    gate_w = pltpu.with_memory_space_constraint(gate_w, pltpu.VMEM)
    up_w = pltpu.with_memory_space_constraint(up_w, pltpu.VMEM)
    down_w = pltpu.with_memory_space_constraint(down_w, pltpu.VMEM)
    tokens, expert_ids, scores = [
        pltpu.with_memory_space_constraint(x, pltpu.HBM) for x in (tokens, expert_ids, scores)
    ]
    packed = pl.pallas_call(
        lambda *refs: pack_kernel(experts, *refs),
        out_shape=jax.ShapeDtypeStruct((rows, width + LANES), jnp.bfloat16),
        in_specs=hbm(3),
        out_specs=vmem(1)[0],
        scratch_shapes=[
            pltpu.VMEM(expert_ids.shape, expert_ids.dtype),
            pltpu.VMEM(scores.shape, scores.dtype),
            pltpu.SemaphoreType.DMA((3,)),
        ],
        compiler_params=params,
        cost_estimate=pl.CostEstimate(
            flops=40_000_000_000, bytes_accessed=100_000_000, transcendentals=0
        ),
        name="pack",
    )(tokens, expert_ids, scores)
    near = join([packed, swap(packed, far)], params)
    pieces = [near] + [swap(near, d) for d in middle]
    pieces = pieces + [swap(piece, 1) for piece in pieces]
    hidden, weight = pl.pallas_call(
        lambda *refs: hidden_kernel(256, fill, experts, *refs),
        out_shape=[
            jax.ShapeDtypeStruct((2 * half, units), jnp.bfloat16),
            jax.ShapeDtypeStruct((2 * half, LANES), jnp.float32),
        ],
        in_specs=vmem(len(pieces) + 2),
        out_specs=vmem(2),
        compiler_params=params,
        name="hidden",
    )(*pieces, gate_w, up_w)
    parts = PARTS
    keeps, gots = [], []
    for part in range(parts):
        keep, send = pl.pallas_call(
            lambda *refs: down_kernel(256, fill, part * width // parts, *refs),
            out_shape=[
                jax.ShapeDtypeStruct((half, width // parts), jnp.float32),
                jax.ShapeDtypeStruct((half, width // parts), jnp.bfloat16),
            ],
            in_specs=vmem(3),
            out_specs=vmem(2),
            compiler_params=params,
            cost_estimate=pl.CostEstimate(
                flops=2 * fill * units * width // parts,
                bytes_accessed=2 * units * width // parts,
                transcendentals=0,
            ),
            name="down",
        )(hidden, weight, down_w)
        keeps.append(keep)
        gots.append(swap(send, 1))
    keep, *sends = pl.pallas_call(
        lambda *refs: first_add_kernel(parts, *refs),
        out_shape=[jax.ShapeDtypeStruct((2 * rows, width), jnp.float32)]
        + [jax.ShapeDtypeStruct((2 * rows, width), jnp.bfloat16)] * len(middle),
        in_specs=vmem(2 * parts),
        out_specs=vmem(1 + len(middle)),
        compiler_params=params,
        name="first_add",
    )(*keeps, *gots)
    gots = [swap(send, d) for send, d in list(zip(sends, middle))[::-1]]
    keep, send = pl.pallas_call(
        second_add_kernel,
        out_shape=[
            jax.ShapeDtypeStruct((rows, width), jnp.float32),
            jax.ShapeDtypeStruct((rows, width), jnp.bfloat16),
        ],
        in_specs=vmem(1 + len(middle)),
        out_specs=vmem(2),
        compiler_params=params,
        name="second_add",
    )(keep, *gots)
    got = swap(send, far)
    return pl.pallas_call(
        last_kernel,
        out_shape=jax.ShapeDtypeStruct((rows, width), jnp.bfloat16),
        in_specs=vmem(2),
        out_specs=vmem(1)[0],
        compiler_params=params,
        name="last",
    )(keep, got)


def solution(mesh):
    in_specs = (
        P(("groups", "expert", "sub", "pair"), None),
        P(("groups", "expert", "sub", "pair"), None),
        P(("groups", "expert", "sub", "pair"), None),
        P("expert", None, "sub"),
        P("expert", None, "sub"),
        P("expert", None, ("sub", "pair")),
    )
    out_specs = P(("groups", "expert", "sub", "pair"), None)
    whole = mesh.shape["sub"] == 1 and mesh.shape["pair"] == 1 and mesh.shape["expert"] == 16
    body = shards if whole else general_shards
    return jax.shard_map(body, mesh=mesh, in_specs=in_specs, out_specs=out_specs, check_vma=False)
```

```python
import jax
import jax.numpy as jnp
from jax import lax
from jax.experimental import pallas as pl
from jax.experimental.pallas import tpu as pltpu
from jax.sharding import PartitionSpec as P

LANES = 128


def slot_table(ids, count):
    hit = (ids[:, :, None] == jnp.arange(count, dtype=jnp.int32)[None, None, :]).astype(jnp.int32)
    per_row = jnp.sum(hit, axis=1)
    before = jnp.cumsum(per_row, axis=0) - per_row
    slot = jnp.sum(hit * before[:, None, :], axis=2)
    return (hit, slot)


def general_shards(tokens, expert_ids, scores, gate_w, up_w, down_w):
    experts = lax.axis_size("expert")
    sub_count = lax.axis_size("sub")
    pair_count = lax.axis_size("pair")
    sharers = sub_count * pair_count
    row_count = tokens.shape[0]
    top_k = expert_ids.shape[1]
    model_width = tokens.shape[1]
    capacity = min(row_count, row_count * top_k // experts + 1)
    weight_gate = gate_w[0]
    weight_up = up_w[0]
    weight_down = down_w[0]
    unit_count = weight_gate.shape[1]
    slot_range = jnp.arange(capacity, dtype=jnp.int32)
    hit, slot = slot_table(expert_ids, experts)
    in_slot = (slot[:, :, None] == slot_range[None, None, :]).astype(jnp.int32)
    place = jnp.sum(hit[:, :, :, None] * in_slot[:, :, None, :], axis=1).astype(jnp.bfloat16)
    buckets = jnp.einsum("rec,rd->ecd", place, tokens, preferred_element_type=jnp.float32).astype(
        jnp.bfloat16
    )
    received = lax.all_to_all(buckets, "expert", split_axis=0, concat_axis=0, tiled=True)
    flat = received.reshape(experts * capacity, model_width)
    piece = lax.all_gather(flat, "sub", axis=0, tiled=True)
    gate_part = jnp.dot(piece, weight_gate, preferred_element_type=jnp.float32)
    up_part = jnp.dot(piece, weight_up, preferred_element_type=jnp.float32)
    hidden = (jax.nn.silu(gate_part) * up_part).astype(jnp.bfloat16)
    stacked = hidden.reshape(sub_count, 1, experts * capacity, unit_count)
    joined = lax.all_gather(stacked, "pair", axis=1, tiled=True)
    joined = joined.reshape(sharers * experts * capacity, unit_count)
    outputs = jnp.dot(
        lax.all_gather(joined, "sub", axis=1, tiled=True),
        weight_down,
        preferred_element_type=jnp.float32,
    ).astype(jnp.bfloat16)
    outputs = outputs.reshape(sharers, experts, capacity, weight_down.shape[1])
    back = lax.all_to_all(
        lax.all_to_all(outputs, ("sub", "pair"), split_axis=0, concat_axis=3, tiled=True),
        "expert",
        split_axis=1,
        concat_axis=0,
        tiled=True,
    )
    back = back.reshape(experts, capacity, model_width).astype(jnp.float32)
    weight = 2.5 * scores / jnp.sum(scores, axis=1, keepdims=True)
    spread = weight[:, :, None, None] * (hit[:, :, :, None] * in_slot[:, :, None, :]).astype(
        jnp.float32
    )
    mixing = jnp.sum(spread, axis=1)
    total = jnp.einsum(
        "rec,ecd->rd",
        mixing,
        back,
        precision=lax.Precision.HIGHEST,
        preferred_element_type=jnp.float32,
    )
    return total.astype(jnp.bfloat16)


def swap(x, distance):
    count = lax.axis_size("expert")
    return lax.ppermute(x, "expert", [(i, i ^ distance) for i in range(count)])


def vmem(count):
    return [pl.BlockSpec(memory_space=pltpu.VMEM)] * count


def hbm(count):
    return [pl.BlockSpec(memory_space=pltpu.HBM)] * count


def filled(x, rows):
    return jnp.concatenate([x, jnp.zeros((rows - x.shape[0], x.shape[1]), x.dtype)], axis=0)


def pack_kernel(experts, tokens_ref, ids_ref, scores_ref, out_ref, ids_vmem, scores_vmem, sems):
    width = tokens_ref.shape[1]
    ids_copy = pltpu.make_async_copy(ids_ref, ids_vmem, sems.at[0])
    scores_copy = pltpu.make_async_copy(scores_ref, scores_vmem, sems.at[1])
    tokens_copy = pltpu.make_async_copy(tokens_ref, out_ref.at[:, pl.ds(0, width)], sems.at[2])
    ids_copy.start()
    scores_copy.start()
    tokens_copy.start()
    ids_copy.wait()
    scores_copy.wait()
    scores = scores_vmem[...]
    ids = ids_vmem[...]
    weight = 2.5 * scores / jnp.sum(scores, axis=1, keepdims=True)
    lane = lax.broadcasted_iota(jnp.int32, (scores.shape[0], LANES), 1)
    target = lax.rem(lane, experts)
    dense = jnp.zeros((scores.shape[0], LANES), jnp.float32)
    for k in range(scores.shape[1]):
        dense = dense + jnp.where(ids[:, k : k + 1] == target, weight[:, k : k + 1], 0.0)
    high = dense.astype(jnp.bfloat16).astype(jnp.float32)
    both = jnp.where(lane < experts, high, jnp.where(lane < 2 * experts, dense - high, 0.0))
    out_ref[:, width:] = both.astype(jnp.bfloat16)
    tokens_copy.wait()


def join_kernel(*refs):
    out_ref = refs[-1]
    pieces = [ref[...].astype(jnp.float32) for ref in refs[:-1]]
    out_ref[...] = jnp.concatenate(pieces, axis=0).astype(out_ref.dtype)


def join(pieces, params):
    rows = sum(piece.shape[0] for piece in pieces)
    return pl.pallas_call(
        join_kernel,
        out_shape=jax.ShapeDtypeStruct((rows, pieces[0].shape[1]), pieces[0].dtype),
        in_specs=vmem(len(pieces)),
        out_specs=vmem(1)[0],
        compiler_params=params,
        name="join",
    )(*pieces)


def hidden_kernel(step, fill, experts, *refs):
    *x_refs, gate_ref, up_ref, out_ref, weight_ref = refs
    width = gate_ref.shape[1]
    rows = out_ref.shape[0]
    me = lax.axis_index("expert")
    spread = jnp.concatenate([ref[:, width:].astype(jnp.float32) for ref in x_refs], axis=0)
    lane = lax.broadcasted_iota(jnp.int32, spread.shape, 1)
    mine = (lane == me) | (lane == me + experts)
    weight = jnp.sum(jnp.where(mine, spread, 0.0), axis=1, keepdims=True)
    weight_ref[...] = jnp.broadcast_to(weight, weight_ref.shape)
    x = jnp.concatenate([ref[:, :width].astype(jnp.float32) for ref in x_refs], axis=0)
    x = filled(x.astype(jnp.bfloat16), fill)
    for start in range(0, gate_ref.shape[2], step):
        cut = slice(start, start + step)
        gate = jnp.dot(x, gate_ref[0, :, cut], preferred_element_type=jnp.float32)[:rows]
        up = jnp.dot(x, up_ref[0, :, cut], preferred_element_type=jnp.float32)[:rows]
        out_ref[:, cut] = (gate / (1.0 + jnp.exp(-gate)) * up).astype(jnp.bfloat16)


def down_kernel(step, fill, hidden_ref, weight_ref, down_ref, *out_refs):
    keep_refs, send_refs = out_refs[: len(out_refs) // 2], out_refs[len(out_refs) // 2 :]
    hidden = filled(hidden_ref[...], fill)
    weight = weight_ref[:, :1]
    rows = keep_refs[0].shape[0]
    for start in range(0, down_ref.shape[2], step):
        cut = slice(start, start + step)
        out = jnp.dot(hidden, down_ref[0, :, cut], preferred_element_type=jnp.float32)
        part = out[: weight.shape[0]].astype(jnp.bfloat16).astype(jnp.float32) * weight
        for i, ref in enumerate(keep_refs + send_refs):
            ref[:, cut] = part[i * rows : (i + 1) * rows].astype(ref.dtype)


def add_kernel(kept_ref, got_ref, out_ref):
    out_ref[...] = (kept_ref[...] + got_ref[...].astype(jnp.float32)).astype(out_ref.dtype)


def fold_kernel(kept_ref, *refs):
    got_refs, (keep_ref, send_ref) = refs[:-2], refs[-2:]
    total = kept_ref[...]
    for got_ref in got_refs:
        total = total + got_ref[...].astype(jnp.float32)
    half = keep_ref.shape[0]
    keep_ref[...] = total[:half]
    send_ref[...] = total[half:].astype(send_ref.dtype)


def add(kept, got, params):
    return pl.pallas_call(
        add_kernel,
        out_shape=jax.ShapeDtypeStruct(got.shape, got.dtype),
        in_specs=vmem(2),
        out_specs=vmem(1)[0],
        compiler_params=params,
        name="add",
    )(kept, got)


def shards(tokens, expert_ids, scores, gate_w, up_w, down_w):
    experts = lax.axis_size("expert")
    rows, width = tokens.shape
    units = gate_w.shape[2]
    far = experts // 2
    middle = [d for d in range(2, far, 2)]
    half = rows * far
    fill = max(2 * half, 128)
    params = pltpu.CompilerParams(vmem_limit_bytes=6 * 2**20)
    gate_w = pltpu.with_memory_space_constraint(gate_w, pltpu.VMEM)
    up_w = pltpu.with_memory_space_constraint(up_w, pltpu.VMEM)
    down_w = pltpu.with_memory_space_constraint(down_w, pltpu.VMEM)
    tokens, expert_ids, scores = [
        pltpu.with_memory_space_constraint(x, pltpu.HBM) for x in (tokens, expert_ids, scores)
    ]
    packed = pl.pallas_call(
        lambda *refs: pack_kernel(experts, *refs),
        out_shape=jax.ShapeDtypeStruct((rows, width + LANES), jnp.bfloat16),
        in_specs=hbm(3),
        out_specs=vmem(1)[0],
        scratch_shapes=[
            pltpu.VMEM(expert_ids.shape, expert_ids.dtype),
            pltpu.VMEM(scores.shape, scores.dtype),
            pltpu.SemaphoreType.DMA((3,)),
        ],
        compiler_params=params,
        cost_estimate=pl.CostEstimate(
            flops=40_000_000_000, bytes_accessed=100_000_000, transcendentals=0
        ),
        name="pack",
    )(tokens, expert_ids, scores)
    near = join([packed, swap(packed, far)], params)
    pieces = [near] + [swap(near, d) for d in middle]
    pieces = pieces + [swap(piece, 1) for piece in pieces]
    hidden, weight = pl.pallas_call(
        lambda *refs: hidden_kernel(256, fill, experts, *refs),
        out_shape=[
            jax.ShapeDtypeStruct((2 * half, units), jnp.bfloat16),
            jax.ShapeDtypeStruct((2 * half, LANES), jnp.float32),
        ],
        in_specs=vmem(len(pieces) + 2),
        out_specs=vmem(2),
        compiler_params=params,
        name="hidden",
    )(*pieces, gate_w, up_w)
    count = len(middle) + 1
    kept_and_sent = pl.pallas_call(
        lambda *refs: down_kernel(256, fill, *refs),
        out_shape=[jax.ShapeDtypeStruct((2 * rows, width), jnp.float32)] * count
        + [jax.ShapeDtypeStruct((2 * rows, width), jnp.bfloat16)] * count,
        in_specs=vmem(3),
        out_specs=vmem(2 * count),
        compiler_params=params,
        name="down",
    )(hidden, weight, down_w)
    kept, sent = kept_and_sent[:count], kept_and_sent[count:]
    gots = [
        swap(add(kept[i], swap(sent[i], 1), params), middle[i - 1]) for i in range(count - 1, 0, -1)
    ]
    gots.append(swap(sent[0], 1))
    keep, send = pl.pallas_call(
        fold_kernel,
        out_shape=[
            jax.ShapeDtypeStruct((rows, width), jnp.float32),
            jax.ShapeDtypeStruct((rows, width), jnp.bfloat16),
        ],
        in_specs=vmem(1 + count),
        out_specs=vmem(2),
        compiler_params=params,
        name="fold",
    )(kept[0], *gots)
    return add(keep, swap(send, far), params)


def solution(mesh):
    in_specs = (
        P(("groups", "expert", "sub", "pair"), None),
        P(("groups", "expert", "sub", "pair"), None),
        P(("groups", "expert", "sub", "pair"), None),
        P("expert", None, "sub"),
        P("expert", None, "sub"),
        P("expert", None, ("sub", "pair")),
    )
    out_specs = P(("groups", "expert", "sub", "pair"), None)
    whole = mesh.shape["sub"] == 1 and mesh.shape["pair"] == 1 and mesh.shape["expert"] == 16
    body = shards if whole else general_shards
    return jax.shard_map(body, mesh=mesh, in_specs=in_specs, out_specs=out_specs, check_vma=False)
```

```python
import jax
import jax.numpy as jnp
from jax import lax
from jax.experimental import pallas as pl
from jax.experimental.pallas import tpu as pltpu
from jax.sharding import PartitionSpec as P

LANES = 128


def slot_table(ids, count):
    hit = (ids[:, :, None] == jnp.arange(count, dtype=jnp.int32)[None, None, :]).astype(jnp.int32)
    per_row = jnp.sum(hit, axis=1)
    before = jnp.cumsum(per_row, axis=0) - per_row
    slot = jnp.sum(hit * before[:, None, :], axis=2)
    return (hit, slot)


def general_shards(tokens, expert_ids, scores, gate_w, up_w, down_w):
    experts = lax.axis_size("expert")
    sub_count = lax.axis_size("sub")
    pair_count = lax.axis_size("pair")
    sharers = sub_count * pair_count
    row_count = tokens.shape[0]
    top_k = expert_ids.shape[1]
    model_width = tokens.shape[1]
    capacity = min(row_count, row_count * top_k // experts + 1)
    weight_gate = gate_w[0]
    weight_up = up_w[0]
    weight_down = down_w[0]
    unit_count = weight_gate.shape[1]
    slot_range = jnp.arange(capacity, dtype=jnp.int32)
    hit, slot = slot_table(expert_ids, experts)
    in_slot = (slot[:, :, None] == slot_range[None, None, :]).astype(jnp.int32)
    place = jnp.sum(hit[:, :, :, None] * in_slot[:, :, None, :], axis=1).astype(jnp.bfloat16)
    buckets = jnp.einsum("rec,rd->ecd", place, tokens, preferred_element_type=jnp.float32).astype(
        jnp.bfloat16
    )
    received = lax.all_to_all(buckets, "expert", split_axis=0, concat_axis=0, tiled=True)
    flat = received.reshape(experts * capacity, model_width)
    piece = lax.all_gather(flat, "sub", axis=0, tiled=True)
    gate_part = jnp.dot(piece, weight_gate, preferred_element_type=jnp.float32)
    up_part = jnp.dot(piece, weight_up, preferred_element_type=jnp.float32)
    hidden = (jax.nn.silu(gate_part) * up_part).astype(jnp.bfloat16)
    stacked = hidden.reshape(sub_count, 1, experts * capacity, unit_count)
    joined = lax.all_gather(stacked, "pair", axis=1, tiled=True)
    joined = joined.reshape(sharers * experts * capacity, unit_count)
    outputs = jnp.dot(
        lax.all_gather(joined, "sub", axis=1, tiled=True),
        weight_down,
        preferred_element_type=jnp.float32,
    ).astype(jnp.bfloat16)
    outputs = outputs.reshape(sharers, experts, capacity, weight_down.shape[1])
    back = lax.all_to_all(
        lax.all_to_all(outputs, ("sub", "pair"), split_axis=0, concat_axis=3, tiled=True),
        "expert",
        split_axis=1,
        concat_axis=0,
        tiled=True,
    )
    back = back.reshape(experts, capacity, model_width).astype(jnp.float32)
    weight = 2.5 * scores / jnp.sum(scores, axis=1, keepdims=True)
    spread = weight[:, :, None, None] * (hit[:, :, :, None] * in_slot[:, :, None, :]).astype(
        jnp.float32
    )
    mixing = jnp.sum(spread, axis=1)
    total = jnp.einsum(
        "rec,ecd->rd",
        mixing,
        back,
        precision=lax.Precision.HIGHEST,
        preferred_element_type=jnp.float32,
    )
    return total.astype(jnp.bfloat16)


def swap(x, distance):
    count = lax.axis_size("expert")
    return lax.ppermute(x, "expert", [(i, i ^ distance) for i in range(count)])


def vmem(count):
    return [pl.BlockSpec(memory_space=pltpu.VMEM)] * count


def hbm(count):
    return [pl.BlockSpec(memory_space=pltpu.HBM)] * count


def filled(x, rows):
    return jnp.concatenate([x, jnp.zeros((rows - x.shape[0], x.shape[1]), x.dtype)], axis=0)


def pack_kernel(experts, tokens_ref, ids_ref, scores_ref, out_ref, ids_vmem, scores_vmem, sems):
    width = tokens_ref.shape[1]
    ids_copy = pltpu.make_async_copy(ids_ref, ids_vmem, sems.at[0])
    scores_copy = pltpu.make_async_copy(scores_ref, scores_vmem, sems.at[1])
    tokens_copy = pltpu.make_async_copy(tokens_ref, out_ref.at[:, pl.ds(0, width)], sems.at[2])
    ids_copy.start()
    scores_copy.start()
    tokens_copy.start()
    ids_copy.wait()
    scores_copy.wait()
    scores = scores_vmem[...]
    ids = ids_vmem[...]
    weight = 2.5 * scores / jnp.sum(scores, axis=1, keepdims=True)
    lane = lax.broadcasted_iota(jnp.int32, (scores.shape[0], LANES), 1)
    target = lax.rem(lane, experts)
    dense = jnp.zeros((scores.shape[0], LANES), jnp.float32)
    for k in range(scores.shape[1]):
        dense = dense + jnp.where(ids[:, k : k + 1] == target, weight[:, k : k + 1], 0.0)
    high = dense.astype(jnp.bfloat16).astype(jnp.float32)
    both = jnp.where(lane < experts, high, jnp.where(lane < 2 * experts, dense - high, 0.0))
    out_ref[:, width:] = both.astype(jnp.bfloat16)
    tokens_copy.wait()


def join_kernel(*refs):
    out_ref = refs[-1]
    pieces = [ref[...].astype(jnp.float32) for ref in refs[:-1]]
    out_ref[...] = jnp.concatenate(pieces, axis=0).astype(out_ref.dtype)


def join(pieces, params):
    rows = sum(piece.shape[0] for piece in pieces)
    return pl.pallas_call(
        join_kernel,
        out_shape=jax.ShapeDtypeStruct((rows, pieces[0].shape[1]), pieces[0].dtype),
        in_specs=vmem(len(pieces)),
        out_specs=vmem(1)[0],
        compiler_params=params,
        name="join",
    )(*pieces)


def expert_kernel(step, fill, experts, count, *refs):
    x_refs, (gate_ref, up_ref, down_ref) = refs[: 2 * count], refs[2 * count : 2 * count + 3]
    out_refs, x_vmem, hidden_vmem = refs[2 * count + 3 : -2], refs[-2], refs[-1]
    width = gate_ref.shape[1]
    units = gate_ref.shape[2]
    me = lax.axis_index("expert")
    spread = jnp.concatenate([ref[:, width:].astype(jnp.float32) for ref in x_refs], axis=0)
    rows = spread.shape[0]
    lane = lax.broadcasted_iota(jnp.int32, spread.shape, 1)
    mine = (lane == me) | (lane == me + experts)
    weight = jnp.sum(jnp.where(mine, spread, 0.0), axis=1, keepdims=True)
    x = jnp.concatenate([ref[:, :width].astype(jnp.float32) for ref in x_refs], axis=0)
    x_vmem[:rows] = x.astype(jnp.bfloat16)
    x_vmem[rows:] = jnp.zeros((fill - rows, width), jnp.bfloat16)
    hidden_vmem[rows:] = jnp.zeros((fill - rows, units), jnp.bfloat16)
    x = x_vmem[...]
    for start in range(0, units, step):
        cut = slice(start, start + step)
        gate = jnp.dot(x, gate_ref[0, :, cut], preferred_element_type=jnp.float32)[:rows]
        up = jnp.dot(x, up_ref[0, :, cut], preferred_element_type=jnp.float32)[:rows]
        hidden_vmem[:rows, cut] = (gate / (1.0 + jnp.exp(-gate)) * up).astype(jnp.bfloat16)
    hidden = hidden_vmem[...]
    for start in range(0, width, step):
        cut = slice(start, start + step)
        out = jnp.dot(hidden, down_ref[0, :, cut], preferred_element_type=jnp.float32)
        part = out[:rows].astype(jnp.bfloat16).astype(jnp.float32) * weight
        piece = out_refs[0].shape[0]
        for i, ref in enumerate(out_refs):
            ref[:, cut] = part[i * piece : (i + 1) * piece].astype(ref.dtype)


def add_kernel(kept_ref, got_ref, out_ref):
    out_ref[...] = (kept_ref[...] + got_ref[...].astype(jnp.float32)).astype(out_ref.dtype)


def fold_kernel(kept_ref, *refs):
    got_refs, (keep_ref, send_ref) = refs[:-2], refs[-2:]
    total = kept_ref[...]
    for got_ref in got_refs:
        total = total + got_ref[...].astype(jnp.float32)
    half = keep_ref.shape[0]
    keep_ref[...] = total[:half]
    send_ref[...] = total[half:].astype(send_ref.dtype)


def add(kept, got, params):
    return pl.pallas_call(
        add_kernel,
        out_shape=jax.ShapeDtypeStruct(got.shape, got.dtype),
        in_specs=vmem(2),
        out_specs=vmem(1)[0],
        compiler_params=params,
        name="add",
    )(kept, got)


def shards(tokens, expert_ids, scores, gate_w, up_w, down_w):
    experts = lax.axis_size("expert")
    rows, width = tokens.shape
    units = gate_w.shape[2]
    far = experts // 2
    middle = [d for d in range(2, far, 2)]
    half = rows * far
    fill = max(2 * half, 128)
    params = pltpu.CompilerParams(vmem_limit_bytes=6 * 2**20)
    gate_w = pltpu.with_memory_space_constraint(gate_w, pltpu.VMEM)
    up_w = pltpu.with_memory_space_constraint(up_w, pltpu.VMEM)
    down_w = pltpu.with_memory_space_constraint(down_w, pltpu.VMEM)
    tokens, expert_ids, scores = [
        pltpu.with_memory_space_constraint(x, pltpu.HBM) for x in (tokens, expert_ids, scores)
    ]
    packed = pl.pallas_call(
        lambda *refs: pack_kernel(experts, *refs),
        out_shape=jax.ShapeDtypeStruct((rows, width + LANES), jnp.bfloat16),
        in_specs=hbm(3),
        out_specs=vmem(1)[0],
        scratch_shapes=[
            pltpu.VMEM(expert_ids.shape, expert_ids.dtype),
            pltpu.VMEM(scores.shape, scores.dtype),
            pltpu.SemaphoreType.DMA((3,)),
        ],
        compiler_params=params,
        cost_estimate=pl.CostEstimate(
            flops=40_000_000_000, bytes_accessed=100_000_000, transcendentals=0
        ),
        name="pack",
    )(tokens, expert_ids, scores)
    near = join([packed, swap(packed, far)], params)
    pieces = [near] + [swap(near, d) for d in middle]
    pieces = pieces + [swap(piece, 1) for piece in pieces]
    count = len(middle) + 1
    kept_and_sent = pl.pallas_call(
        lambda *refs: expert_kernel(256, fill, experts, count, *refs),
        out_shape=[jax.ShapeDtypeStruct((2 * rows, width), jnp.float32)] * count
        + [jax.ShapeDtypeStruct((2 * rows, width), jnp.bfloat16)] * count,
        in_specs=vmem(2 * count + 3),
        out_specs=vmem(2 * count),
        scratch_shapes=[
            pltpu.VMEM((fill, width), jnp.bfloat16),
            pltpu.VMEM((fill, units), jnp.bfloat16),
        ],
        compiler_params=params,
        name="expert",
    )(*pieces, gate_w, up_w, down_w)
    kept, sent = kept_and_sent[:count], kept_and_sent[count:]
    gots = [
        swap(add(kept[i], swap(sent[i], 1), params), middle[i - 1]) for i in range(count - 1, 0, -1)
    ]
    gots.append(swap(sent[0], 1))
    keep, send = pl.pallas_call(
        fold_kernel,
        out_shape=[
            jax.ShapeDtypeStruct((rows, width), jnp.float32),
            jax.ShapeDtypeStruct((rows, width), jnp.bfloat16),
        ],
        in_specs=vmem(1 + count),
        out_specs=vmem(2),
        compiler_params=params,
        name="fold",
    )(kept[0], *gots)
    return add(keep, swap(send, far), params)


def solution(mesh):
    in_specs = (
        P(("groups", "expert", "sub", "pair"), None),
        P(("groups", "expert", "sub", "pair"), None),
        P(("groups", "expert", "sub", "pair"), None),
        P("expert", None, "sub"),
        P("expert", None, "sub"),
        P("expert", None, ("sub", "pair")),
    )
    out_specs = P(("groups", "expert", "sub", "pair"), None)
    whole = mesh.shape["sub"] == 1 and mesh.shape["pair"] == 1 and mesh.shape["expert"] == 16
    body = shards if whole else general_shards
    return jax.shard_map(body, mesh=mesh, in_specs=in_specs, out_specs=out_specs, check_vma=False)
```

```python
import jax
import jax.numpy as jnp
from jax import lax
from jax.experimental import pallas as pl
from jax.experimental.pallas import tpu as pltpu
from jax.sharding import PartitionSpec as P

LANES = 128


def slot_table(ids, count):
    hit = (ids[:, :, None] == jnp.arange(count, dtype=jnp.int32)[None, None, :]).astype(jnp.int32)
    per_row = jnp.sum(hit, axis=1)
    before = jnp.cumsum(per_row, axis=0) - per_row
    slot = jnp.sum(hit * before[:, None, :], axis=2)
    return (hit, slot)


def general_shards(tokens, expert_ids, scores, gate_w, up_w, down_w):
    experts = lax.axis_size("expert")
    sub_count = lax.axis_size("sub")
    pair_count = lax.axis_size("pair")
    sharers = sub_count * pair_count
    row_count = tokens.shape[0]
    top_k = expert_ids.shape[1]
    model_width = tokens.shape[1]
    capacity = min(row_count, row_count * top_k // experts + 1)
    weight_gate = gate_w[0]
    weight_up = up_w[0]
    weight_down = down_w[0]
    unit_count = weight_gate.shape[1]
    slot_range = jnp.arange(capacity, dtype=jnp.int32)
    hit, slot = slot_table(expert_ids, experts)
    in_slot = (slot[:, :, None] == slot_range[None, None, :]).astype(jnp.int32)
    place = jnp.sum(hit[:, :, :, None] * in_slot[:, :, None, :], axis=1).astype(jnp.bfloat16)
    buckets = jnp.einsum("rec,rd->ecd", place, tokens, preferred_element_type=jnp.float32).astype(
        jnp.bfloat16
    )
    received = lax.all_to_all(buckets, "expert", split_axis=0, concat_axis=0, tiled=True)
    flat = received.reshape(experts * capacity, model_width)
    piece = lax.all_gather(flat, "sub", axis=0, tiled=True)
    gate_part = jnp.dot(piece, weight_gate, preferred_element_type=jnp.float32)
    up_part = jnp.dot(piece, weight_up, preferred_element_type=jnp.float32)
    hidden = (jax.nn.silu(gate_part) * up_part).astype(jnp.bfloat16)
    stacked = hidden.reshape(sub_count, 1, experts * capacity, unit_count)
    joined = lax.all_gather(stacked, "pair", axis=1, tiled=True)
    joined = joined.reshape(sharers * experts * capacity, unit_count)
    outputs = jnp.dot(
        lax.all_gather(joined, "sub", axis=1, tiled=True),
        weight_down,
        preferred_element_type=jnp.float32,
    ).astype(jnp.bfloat16)
    outputs = outputs.reshape(sharers, experts, capacity, weight_down.shape[1])
    back = lax.all_to_all(
        lax.all_to_all(outputs, ("sub", "pair"), split_axis=0, concat_axis=3, tiled=True),
        "expert",
        split_axis=1,
        concat_axis=0,
        tiled=True,
    )
    back = back.reshape(experts, capacity, model_width).astype(jnp.float32)
    weight = 2.5 * scores / jnp.sum(scores, axis=1, keepdims=True)
    spread = weight[:, :, None, None] * (hit[:, :, :, None] * in_slot[:, :, None, :]).astype(
        jnp.float32
    )
    mixing = jnp.sum(spread, axis=1)
    total = jnp.einsum(
        "rec,ecd->rd",
        mixing,
        back,
        precision=lax.Precision.HIGHEST,
        preferred_element_type=jnp.float32,
    )
    return total.astype(jnp.bfloat16)


def swap(x, distance):
    count = lax.axis_size("expert")
    return lax.ppermute(x, "expert", [(i, i ^ distance) for i in range(count)])


def vmem(count):
    return [pl.BlockSpec(memory_space=pltpu.VMEM)] * count


def hbm(count):
    return [pl.BlockSpec(memory_space=pltpu.HBM)] * count


def filled(x, rows):
    return jnp.concatenate([x, jnp.zeros((rows - x.shape[0], x.shape[1]), x.dtype)], axis=0)


def pack_kernel(experts, tokens_ref, ids_ref, scores_ref, out_ref, ids_vmem, scores_vmem, sems):
    width = tokens_ref.shape[1]
    ids_copy = pltpu.make_async_copy(ids_ref, ids_vmem, sems.at[0])
    scores_copy = pltpu.make_async_copy(scores_ref, scores_vmem, sems.at[1])
    tokens_copy = pltpu.make_async_copy(tokens_ref, out_ref.at[:, pl.ds(0, width)], sems.at[2])
    ids_copy.start()
    scores_copy.start()
    tokens_copy.start()
    ids_copy.wait()
    scores_copy.wait()
    scores = scores_vmem[...]
    ids = ids_vmem[...]
    weight = 2.5 * scores / jnp.sum(scores, axis=1, keepdims=True)
    lane = lax.broadcasted_iota(jnp.int32, (scores.shape[0], LANES), 1)
    target = lax.rem(lane, experts)
    dense = jnp.zeros((scores.shape[0], LANES), jnp.float32)
    for k in range(scores.shape[1]):
        dense = dense + jnp.where(ids[:, k : k + 1] == target, weight[:, k : k + 1], 0.0)
    high = dense.astype(jnp.bfloat16).astype(jnp.float32)
    both = jnp.where(lane < experts, high, jnp.where(lane < 2 * experts, dense - high, 0.0))
    out_ref[:, width:] = both.astype(jnp.bfloat16)
    tokens_copy.wait()


def join_kernel(*refs):
    out_ref = refs[-1]
    pieces = [ref[...].astype(jnp.float32) for ref in refs[:-1]]
    out_ref[...] = jnp.concatenate(pieces, axis=0).astype(out_ref.dtype)


def join(pieces, params):
    rows = sum(piece.shape[0] for piece in pieces)
    return pl.pallas_call(
        join_kernel,
        out_shape=jax.ShapeDtypeStruct((rows, pieces[0].shape[1]), pieces[0].dtype),
        in_specs=vmem(len(pieces)),
        out_specs=vmem(1)[0],
        compiler_params=params,
        name="join",
    )(*pieces)


def expert_kernel(step, fill, experts, count, *refs):
    x_refs, (gate_ref, up_ref, down_ref) = refs[: 2 * count], refs[2 * count : 2 * count + 3]
    out_refs, x_vmem, hidden_vmem = refs[2 * count + 3 : -2], refs[-2], refs[-1]
    width = gate_ref.shape[1]
    units = gate_ref.shape[2]
    me = lax.axis_index("expert")
    spread = jnp.concatenate([ref[:, width:].astype(jnp.float32) for ref in x_refs], axis=0)
    rows = spread.shape[0]
    lane = lax.broadcasted_iota(jnp.int32, spread.shape, 1)
    mine = (lane == me) | (lane == me + experts)
    weight = jnp.sum(jnp.where(mine, spread, 0.0), axis=1, keepdims=True)
    x = jnp.concatenate([ref[:, :width].astype(jnp.float32) for ref in x_refs], axis=0)
    x_vmem[:rows] = x.astype(jnp.bfloat16)
    x_vmem[rows:] = jnp.zeros((fill - rows, width), jnp.bfloat16)
    hidden_vmem[rows:] = jnp.zeros((fill - rows, units), jnp.bfloat16)
    x = x_vmem[...]
    for start in range(0, units, step):
        cut = slice(start, start + step)
        gate = jnp.dot(x, gate_ref[0, :, cut], preferred_element_type=jnp.float32)[:rows]
        up = jnp.dot(x, up_ref[0, :, cut], preferred_element_type=jnp.float32)[:rows]
        hidden_vmem[:rows, cut] = (gate / (1.0 + jnp.exp(-gate)) * up).astype(jnp.bfloat16)
    hidden = hidden_vmem[...]
    for start in range(0, width, step):
        cut = slice(start, start + step)
        out = jnp.dot(hidden, down_ref[0, :, cut], preferred_element_type=jnp.float32)
        part = out[:rows].astype(jnp.bfloat16).astype(jnp.float32) * weight
        piece = out_refs[0].shape[0]
        for i, ref in enumerate(out_refs):
            ref[:, cut] = part[i * piece : (i + 1) * piece].astype(ref.dtype)


def add_kernel(kept_ref, got_ref, out_ref):
    out_ref[...] = (kept_ref[...] + got_ref[...].astype(jnp.float32)).astype(out_ref.dtype)


def fold_kernel(kept_ref, *refs):
    got_refs, (keep_ref, send_ref) = refs[:-2], refs[-2:]
    total = kept_ref[...]
    for got_ref in got_refs:
        total = total + got_ref[...].astype(jnp.float32)
    half = keep_ref.shape[0]
    keep_ref[...] = total[:half]
    send_ref[...] = total[half:].astype(send_ref.dtype)


def add(kept, got, params):
    return pl.pallas_call(
        add_kernel,
        out_shape=jax.ShapeDtypeStruct(got.shape, got.dtype),
        in_specs=vmem(2),
        out_specs=vmem(1)[0],
        compiler_params=params,
        name="add",
    )(kept, got)


def shards(tokens, expert_ids, scores, gate_w, up_w, down_w):
    experts = lax.axis_size("expert")
    rows, width = tokens.shape
    units = gate_w.shape[2]
    far = experts // 2 + 1
    middle = [d + 1 for d in range(2, far - 1, 2)]
    half = rows * experts // 2
    fill = max(2 * half, 128)
    params = pltpu.CompilerParams(vmem_limit_bytes=6 * 2**20)
    gate_w = pltpu.with_memory_space_constraint(gate_w, pltpu.VMEM)
    up_w = pltpu.with_memory_space_constraint(up_w, pltpu.VMEM)
    down_w = pltpu.with_memory_space_constraint(down_w, pltpu.VMEM)
    tokens, expert_ids, scores = [
        pltpu.with_memory_space_constraint(x, pltpu.HBM) for x in (tokens, expert_ids, scores)
    ]
    packed = pl.pallas_call(
        lambda *refs: pack_kernel(experts, *refs),
        out_shape=jax.ShapeDtypeStruct((rows, width + LANES), jnp.bfloat16),
        in_specs=hbm(3),
        out_specs=vmem(1)[0],
        scratch_shapes=[
            pltpu.VMEM(expert_ids.shape, expert_ids.dtype),
            pltpu.VMEM(scores.shape, scores.dtype),
            pltpu.SemaphoreType.DMA((3,)),
        ],
        compiler_params=params,
        cost_estimate=pl.CostEstimate(
            flops=40_000_000_000, bytes_accessed=100_000_000, transcendentals=0
        ),
        name="pack",
    )(tokens, expert_ids, scores)
    near = join([packed, swap(packed, far)], params)
    pieces = [near] + [swap(near, d) for d in middle]
    pieces = pieces + [swap(piece, 1) for piece in pieces]
    count = len(middle) + 1
    kept_and_sent = pl.pallas_call(
        lambda *refs: expert_kernel(256, fill, experts, count, *refs),
        out_shape=[jax.ShapeDtypeStruct((2 * rows, width), jnp.float32)] * count
        + [jax.ShapeDtypeStruct((2 * rows, width), jnp.bfloat16)] * count,
        in_specs=vmem(2 * count + 3),
        out_specs=vmem(2 * count),
        scratch_shapes=[
            pltpu.VMEM((fill, width), jnp.bfloat16),
            pltpu.VMEM((fill, units), jnp.bfloat16),
        ],
        compiler_params=params,
        name="expert",
    )(*pieces, gate_w, up_w, down_w)
    kept, sent = kept_and_sent[:count], kept_and_sent[count:]
    gots = [
        swap(add(kept[i], swap(sent[i], 1), params), middle[i - 1]) for i in range(count - 1, 0, -1)
    ]
    gots.append(swap(sent[0], 1))
    keep, send = pl.pallas_call(
        fold_kernel,
        out_shape=[
            jax.ShapeDtypeStruct((rows, width), jnp.float32),
            jax.ShapeDtypeStruct((rows, width), jnp.bfloat16),
        ],
        in_specs=vmem(1 + count),
        out_specs=vmem(2),
        compiler_params=params,
        name="fold",
    )(kept[0], *gots)
    return add(keep, swap(send, far), params)


def solution(mesh):
    in_specs = (
        P(("groups", "expert", "sub", "pair"), None),
        P(("groups", "expert", "sub", "pair"), None),
        P(("groups", "expert", "sub", "pair"), None),
        P("expert", None, "sub"),
        P("expert", None, "sub"),
        P("expert", None, ("sub", "pair")),
    )
    out_specs = P(("groups", "expert", "sub", "pair"), None)
    whole = mesh.shape["sub"] == 1 and mesh.shape["pair"] == 1 and mesh.shape["expert"] == 16
    body = shards if whole else general_shards
    return jax.shard_map(body, mesh=mesh, in_specs=in_specs, out_specs=out_specs, check_vma=False)
```

```python
import jax
import jax.numpy as jnp
from jax import lax
from jax.experimental import pallas as pl
from jax.experimental.pallas import tpu as pltpu
from jax.sharding import PartitionSpec as P

LANES = 128


def slot_table(ids, count):
    hit = (ids[:, :, None] == jnp.arange(count, dtype=jnp.int32)[None, None, :]).astype(jnp.int32)
    per_row = jnp.sum(hit, axis=1)
    before = jnp.cumsum(per_row, axis=0) - per_row
    slot = jnp.sum(hit * before[:, None, :], axis=2)
    return (hit, slot)


def general_shards(tokens, expert_ids, scores, gate_w, up_w, down_w):
    experts = lax.axis_size("expert")
    sub_count = lax.axis_size("sub")
    pair_count = lax.axis_size("pair")
    sharers = sub_count * pair_count
    row_count = tokens.shape[0]
    top_k = expert_ids.shape[1]
    model_width = tokens.shape[1]
    capacity = min(row_count, row_count * top_k // experts + 1)
    weight_gate = gate_w[0]
    weight_up = up_w[0]
    weight_down = down_w[0]
    unit_count = weight_gate.shape[1]
    slot_range = jnp.arange(capacity, dtype=jnp.int32)
    hit, slot = slot_table(expert_ids, experts)
    in_slot = (slot[:, :, None] == slot_range[None, None, :]).astype(jnp.int32)
    place = jnp.sum(hit[:, :, :, None] * in_slot[:, :, None, :], axis=1).astype(jnp.bfloat16)
    buckets = jnp.einsum("rec,rd->ecd", place, tokens, preferred_element_type=jnp.float32).astype(
        jnp.bfloat16
    )
    received = lax.all_to_all(buckets, "expert", split_axis=0, concat_axis=0, tiled=True)
    flat = received.reshape(experts * capacity, model_width)
    piece = lax.all_gather(flat, "sub", axis=0, tiled=True)
    gate_part = jnp.dot(piece, weight_gate, preferred_element_type=jnp.float32)
    up_part = jnp.dot(piece, weight_up, preferred_element_type=jnp.float32)
    hidden = (jax.nn.silu(gate_part) * up_part).astype(jnp.bfloat16)
    stacked = hidden.reshape(sub_count, 1, experts * capacity, unit_count)
    joined = lax.all_gather(stacked, "pair", axis=1, tiled=True)
    joined = joined.reshape(sharers * experts * capacity, unit_count)
    outputs = jnp.dot(
        lax.all_gather(joined, "sub", axis=1, tiled=True),
        weight_down,
        preferred_element_type=jnp.float32,
    ).astype(jnp.bfloat16)
    outputs = outputs.reshape(sharers, experts, capacity, weight_down.shape[1])
    back = lax.all_to_all(
        lax.all_to_all(outputs, ("sub", "pair"), split_axis=0, concat_axis=3, tiled=True),
        "expert",
        split_axis=1,
        concat_axis=0,
        tiled=True,
    )
    back = back.reshape(experts, capacity, model_width).astype(jnp.float32)
    weight = 2.5 * scores / jnp.sum(scores, axis=1, keepdims=True)
    spread = weight[:, :, None, None] * (hit[:, :, :, None] * in_slot[:, :, None, :]).astype(
        jnp.float32
    )
    mixing = jnp.sum(spread, axis=1)
    total = jnp.einsum(
        "rec,ecd->rd",
        mixing,
        back,
        precision=lax.Precision.HIGHEST,
        preferred_element_type=jnp.float32,
    )
    return total.astype(jnp.bfloat16)


def swap(x, distance):
    count = lax.axis_size("expert")
    return lax.ppermute(x, "expert", [(i, i ^ distance) for i in range(count)])


def vmem(count):
    return [pl.BlockSpec(memory_space=pltpu.VMEM)] * count


def hbm(count):
    return [pl.BlockSpec(memory_space=pltpu.HBM)] * count


def filled(x, rows):
    return jnp.concatenate([x, jnp.zeros((rows - x.shape[0], x.shape[1]), x.dtype)], axis=0)


def pack_kernel(experts, tokens_ref, ids_ref, scores_ref, out_ref, ids_vmem, scores_vmem, sems):
    width = tokens_ref.shape[1]
    ids_copy = pltpu.make_async_copy(ids_ref, ids_vmem, sems.at[0])
    scores_copy = pltpu.make_async_copy(scores_ref, scores_vmem, sems.at[1])
    tokens_copy = pltpu.make_async_copy(tokens_ref, out_ref.at[:, pl.ds(0, width)], sems.at[2])
    ids_copy.start()
    scores_copy.start()
    tokens_copy.start()
    ids_copy.wait()
    scores_copy.wait()
    scores = scores_vmem[...]
    ids = ids_vmem[...]
    weight = 2.5 * scores / jnp.sum(scores, axis=1, keepdims=True)
    lane = lax.broadcasted_iota(jnp.int32, (scores.shape[0], LANES), 1)
    target = lax.rem(lane, experts)
    dense = jnp.zeros((scores.shape[0], LANES), jnp.float32)
    for k in range(scores.shape[1]):
        dense = dense + jnp.where(ids[:, k : k + 1] == target, weight[:, k : k + 1], 0.0)
    high = dense.astype(jnp.bfloat16).astype(jnp.float32)
    both = jnp.where(lane < experts, high, jnp.where(lane < 2 * experts, dense - high, 0.0))
    out_ref[:, width:] = both.astype(jnp.bfloat16)
    tokens_copy.wait()


def join_kernel(*refs):
    out_ref = refs[-1]
    pieces = [ref[...].astype(jnp.float32) for ref in refs[:-1]]
    out_ref[...] = jnp.concatenate(pieces, axis=0).astype(out_ref.dtype)


def join(pieces, params):
    rows = sum(piece.shape[0] for piece in pieces)
    return pl.pallas_call(
        join_kernel,
        out_shape=jax.ShapeDtypeStruct((rows, pieces[0].shape[1]), pieces[0].dtype),
        in_specs=vmem(len(pieces)),
        out_specs=vmem(1)[0],
        compiler_params=params,
        name="join",
    )(*pieces)


def hidden_kernel(step, fill, experts, *refs):
    *x_refs, gate_ref, up_ref, out_ref, weight_ref = refs
    width = gate_ref.shape[1]
    rows = out_ref.shape[0]
    me = lax.axis_index("expert")
    spread = jnp.concatenate([ref[:, width:].astype(jnp.float32) for ref in x_refs], axis=0)
    lane = lax.broadcasted_iota(jnp.int32, spread.shape, 1)
    mine = (lane == me) | (lane == me + experts)
    weight = jnp.sum(jnp.where(mine, spread, 0.0), axis=1, keepdims=True)
    weight_ref[...] = jnp.broadcast_to(weight, weight_ref.shape)
    x = jnp.concatenate([ref[:, :width].astype(jnp.float32) for ref in x_refs], axis=0)
    x = filled(x.astype(jnp.bfloat16), fill)
    for start in range(0, gate_ref.shape[2], step):
        cut = slice(start, start + step)
        gate = jnp.dot(x, gate_ref[0, :, cut], preferred_element_type=jnp.float32)[:rows]
        up = jnp.dot(x, up_ref[0, :, cut], preferred_element_type=jnp.float32)[:rows]
        out_ref[:, cut] = (gate / (1.0 + jnp.exp(-gate)) * up).astype(jnp.bfloat16)


def down_kernel(step, fill, hidden_ref, weight_ref, down_ref, *out_refs):
    hidden = filled(hidden_ref[...], fill)
    weight = weight_ref[:, :1]
    for start in range(0, down_ref.shape[2], step):
        cut = slice(start, start + step)
        out = jnp.dot(hidden, down_ref[0, :, cut], preferred_element_type=jnp.float32)
        part = out[: weight.shape[0]].astype(jnp.bfloat16).astype(jnp.float32) * weight
        base = 0
        for ref in out_refs:
            ref[:, cut] = part[base : base + ref.shape[0]].astype(ref.dtype)
            base += ref.shape[0]


def split_kernel(kept_ref, got_ref, *out_refs):
    total = kept_ref[...] + got_ref[...].astype(jnp.float32)
    base = 0
    for ref in out_refs:
        ref[...] = total[base : base + ref.shape[0]].astype(ref.dtype)
        base += ref.shape[0]


def add_kernel(kept_ref, got_ref, out_ref):
    out_ref[...] = (kept_ref[...] + got_ref[...].astype(jnp.float32)).astype(out_ref.dtype)


def fold_kernel(*refs):
    got_refs, (kept_ref, keep_ref, send_ref) = refs[:-3], refs[-3:]
    total = kept_ref[...]
    for got_ref in got_refs:
        total = total + got_ref[...].astype(jnp.float32)
    half = keep_ref.shape[0]
    keep_ref[...] = total[:half]
    send_ref[...] = total[half:].astype(send_ref.dtype)


def split(kept, got, dtypes, params):
    rows, width = kept.shape
    return pl.pallas_call(
        split_kernel,
        out_shape=[jax.ShapeDtypeStruct((rows // len(dtypes), width), dtype) for dtype in dtypes],
        in_specs=vmem(2),
        out_specs=vmem(len(dtypes)),
        compiler_params=params,
        name="split",
    )(kept, got)


def add(kept, got, params):
    return pl.pallas_call(
        add_kernel,
        out_shape=jax.ShapeDtypeStruct(got.shape, got.dtype),
        in_specs=vmem(2),
        out_specs=vmem(1)[0],
        compiler_params=params,
        name="add",
    )(kept, got)


def shards(tokens, expert_ids, scores, gate_w, up_w, down_w):
    experts = lax.axis_size("expert")
    rows, width = tokens.shape
    units = gate_w.shape[2]
    far = experts // 2 + 1
    middle = [d + 1 for d in range(2, far - 1, 2)]
    half = rows * experts // 2
    fill = max(2 * half, 128)
    params = pltpu.CompilerParams(vmem_limit_bytes=6 * 2**20)
    gate_w = pltpu.with_memory_space_constraint(gate_w, pltpu.VMEM)
    up_w = pltpu.with_memory_space_constraint(up_w, pltpu.VMEM)
    down_w = pltpu.with_memory_space_constraint(down_w, pltpu.VMEM)
    tokens, expert_ids, scores = [
        pltpu.with_memory_space_constraint(x, pltpu.HBM) for x in (tokens, expert_ids, scores)
    ]
    packed = pl.pallas_call(
        lambda *refs: pack_kernel(experts, *refs),
        out_shape=jax.ShapeDtypeStruct((rows, width + LANES), jnp.bfloat16),
        in_specs=hbm(3),
        out_specs=vmem(1)[0],
        scratch_shapes=[
            pltpu.VMEM(expert_ids.shape, expert_ids.dtype),
            pltpu.VMEM(scores.shape, scores.dtype),
            pltpu.SemaphoreType.DMA((3,)),
        ],
        compiler_params=params,
        cost_estimate=pl.CostEstimate(
            flops=40_000_000_000, bytes_accessed=100_000_000, transcendentals=0
        ),
        name="pack",
    )(tokens, expert_ids, scores)
    near = join([packed, swap(packed, far)], params)
    pieces = [near] + [swap(near, d) for d in middle]
    pieces = pieces + [swap(piece, 1) for piece in pieces]
    hidden, weight = pl.pallas_call(
        lambda *refs: hidden_kernel(256, fill, experts, *refs),
        out_shape=[
            jax.ShapeDtypeStruct((2 * half, units), jnp.bfloat16),
            jax.ShapeDtypeStruct((2 * half, LANES), jnp.float32),
        ],
        in_specs=vmem(len(pieces) + 2),
        out_specs=vmem(2),
        compiler_params=params,
        name="hidden",
    )(*pieces, gate_w, up_w)
    count = len(middle) + 1
    kept_and_sent = pl.pallas_call(
        lambda *refs: down_kernel(256, fill, *refs),
        out_shape=[
            jax.ShapeDtypeStruct((half // 2, width), dtype)
            for dtype in (jnp.float32, jnp.float32, jnp.bfloat16, jnp.bfloat16)
        ],
        in_specs=vmem(3),
        out_specs=vmem(4),
        compiler_params=params,
        name="down",
    )(hidden, weight, down_w)
    kept_low, kept_high, sent_low, sent_high = kept_and_sent
    third, corner = split(kept_high, swap(sent_high, 1), (jnp.bfloat16, jnp.bfloat16), params)
    near, second = split(kept_low, swap(sent_low, 1), (jnp.float32, jnp.bfloat16), params)
    gots = [swap(send, d) for send, d in zip((corner, third, second), middle[::-1])]
    keep, send = pl.pallas_call(
        fold_kernel,
        out_shape=[
            jax.ShapeDtypeStruct((rows, width), jnp.float32),
            jax.ShapeDtypeStruct((rows, width), jnp.bfloat16),
        ],
        in_specs=vmem(count),
        out_specs=vmem(2),
        compiler_params=params,
        name="fold",
    )(*gots, near)
    return add(keep, swap(send, far), params)


def solution(mesh):
    in_specs = (
        P(("groups", "expert", "sub", "pair"), None),
        P(("groups", "expert", "sub", "pair"), None),
        P(("groups", "expert", "sub", "pair"), None),
        P("expert", None, "sub"),
        P("expert", None, "sub"),
        P("expert", None, ("sub", "pair")),
    )
    out_specs = P(("groups", "expert", "sub", "pair"), None)
    whole = mesh.shape["sub"] == 1 and mesh.shape["pair"] == 1 and mesh.shape["expert"] == 16
    body = shards if whole else general_shards
    return jax.shard_map(body, mesh=mesh, in_specs=in_specs, out_specs=out_specs, check_vma=False)
```
